256 devices in a mesh: ctx: 64 (over y, z, core), head: 4 (over x).
Axes of the slice: x: 4, y: 4, z: 8, core: 2. Of those that a mesh axis runs over, the one named last changes fastest.
Arguments:
- queries: bfloat16 [32768, 512], P('ctx', 'head'), may hold values from -400 to 400
- keys: bfloat16 [32768, 128], P('ctx'), may hold values from -4 to 4
- values: bfloat16 [32768, 128], P('ctx'), may hold values from -6 to 6
Outputs:
- attended: bfloat16 [32768, 512], P('ctx', 'head')
The draws below stay inside these ranges and needn't reach their ends.
All inputs are finite; a program needn't handle non-finite values.
Results may differ from the reference program's by a relative error of at most 0.0065.
Values may be sent and summed in bfloat16 or wider, within the bound.
A program may use at most 64 MiB of HBM per device.

```python
import math
import jax
import jax.numpy as jnp
from jax import lax

HD = 128
HQ = 4
TOKENS = 32768


def key_base(key):
    return jnp.clip(jax.random.normal(key, (TOKENS, HD), jnp.float32), -4.0, 4.0)


def draw_keys(key, part):
    base = key_base(key)
    return base.astype(jnp.bfloat16)


def draw_queries(key, part):
    key = jax.random.fold_in(key, 23)
    fresh = jnp.clip(jax.random.normal(key, (TOKENS, HQ * HD), jnp.float32), -4.0, 4.0)
    return fresh.astype(jnp.bfloat16)


def block_scale(key, dims, cuts, smallest, top_value):
    loudness, own = 1.0, jax.random.fold_in(key, 6)
    for dim, parts in cuts:
        steps = jnp.exp(jax.random.uniform(jax.random.fold_in(own, dim), (parts,), jnp.float32, smallest / len(cuts), top_value / len(cuts)))
        loudness = loudness * jnp.repeat(steps, dims[dim] // parts).reshape([-1 if axis == dim else 1 for axis in range(len(dims))])
    return loudness


def scatter_about(key, dims, deviation, bound, pieces=(), held_as=jnp.bfloat16):
    drawn = deviation * jax.random.normal(key, dims, jnp.float32)
    if pieces:
        drawn = drawn * block_scale(key, dims, pieces, -0.22, 0.18)
    return jnp.clip(drawn, -bound, bound).astype(held_as)


def setup_inputs(seed: int = 0) -> dict:
    key_list = jax.random.split(jax.random.key(seed), 4)
    return {
        "queries": draw_queries(jax.random.fold_in(key_list[3], 71), 0),
        "keys": draw_keys(jax.random.fold_in(key_list[3], 71), 0),
        "values": scatter_about(key_list[2], (TOKENS, HD), 1.0, 6.0, ((0, 64),)),
    }


def reference(queries, keys, values):
    block_rows = math.gcd(512, TOKENS)
    score_scale = 1.0 / math.sqrt(HD)
    grouped = queries.reshape(TOKENS // block_rows, block_rows, HQ, HD)
    offsets = jnp.arange(TOKENS // block_rows, dtype=jnp.int32) * block_rows
    key_pos = jnp.arange(TOKENS, dtype=jnp.int32)

    def one_block(inputs):
        query_block, offset = inputs
        query_pos = offset + jnp.arange(block_rows, dtype=jnp.int32)
        visible = key_pos[None, :] <= query_pos[:, None]
        outputs = []
        for head_number in range(HQ):
            scores = jnp.dot(query_block[:, head_number, :], keys.T, preferred_element_type=jnp.float32) * score_scale
            masked = jnp.where(visible, scores, -jnp.inf)
            row_max = lax.optimization_barrier(jnp.max(masked, axis=1))
            weights = jnp.where(visible, jnp.exp(scores - row_max[:, None]), jnp.float32(0.0))
            totals = lax.optimization_barrier(jnp.sum(weights, axis=1))
            summed = jnp.dot(weights.astype(jnp.bfloat16), values, preferred_element_type=jnp.float32)
            outputs.append((summed / totals[:, None]).astype(jnp.bfloat16))
        return jnp.stack(outputs, axis=1)
    result = lax.map(one_block, (grouped, offsets))
    return result.reshape(TOKENS, HQ * HD)
```

```python
import math

import jax
import jax.numpy as jnp
from jax import lax
from jax.experimental import pallas as pl
from jax.experimental.pallas import tpu as pltpu
from jax.sharding import PartitionSpec as P

MESH = pl.DeviceIdType.MESH
NX, NY, NZ = 4, 4, 8
BLK = 128
HD = 128
COLS = NX * BLK
SCALE = math.log2(math.e) / math.sqrt(HD)
EMPTY = -1e30
HIDDEN = -2e30
ORDER = (2, 3, 0, 1)
F32 = jnp.float32
BF16 = jnp.bfloat16


def kernel(
    q_ref, k_ref, v_ref, o_ref,
    kv, qown, qb, s0, s1, s2, s3, mx, mp, ls, acc, osend, orecv,
    rs, zs, ys, yo, ss, sr, qss, qrs, oss, ors,
):
    scores = (s0, s1, s2, s3)
    ctx, x = lax.axis_index("ctx"), lax.axis_index("head")
    c = lax.rem(ctx, 2)
    z = lax.rem(lax.div(ctx, 2), NZ)
    y = lax.div(ctx, 2 * NZ)
    opp = lax.rem(y + 2, NY)
    yup, ydn = lax.rem(y + 1, NY), lax.rem(y + NY - 1, NY)
    zup, zdn = lax.rem(z + 1, NZ), lax.rem(z + NZ - 1, NZ)
    peers = [(dx, dy) for dy in range(NY) for dx in range(NX) if dx or dy]

    def dev(xx, yy, zz, cc):
        return ((yy * NZ + zz) * 2 + cc, xx)

    def copy(src, dst, send, recv, device):
        return pltpu.make_async_remote_copy(
            src_ref=src, dst_ref=dst, send_sem=send, recv_sem=recv, device_id=device, device_id_type=MESH
        )

    barrier = pltpu.get_barrier_semaphore()
    targets = [dev(lax.rem(x + dx, NX), lax.rem(y + dy, NY), z, c) for dx, dy in peers]
    targets += [dev(x, y, zup, c), dev(x, y, zdn, c), dev(x, y, z, 1 - c)]
    for target in targets:
        pl.semaphore_signal(barrier, inc=1, device_id=target, device_id_type=MESH)

    def turn(a):
        return a.astype(F32).T.astype(BF16)

    rows = pl.ds(pl.multiple_of(x * BLK, BLK), BLK)
    for r in range(NY):
        qown[r] = turn(q_ref[r * BLK:(r + 1) * BLK, :])
    qb[y, x] = qown[y]
    kv[z, c, y, :BLK, :] = k_ref[rows, :]
    kv[z, c, y, BLK:, :] = turn(v_ref[rows, :])
    for g in range(NY):
        mx[g] = jnp.full((1, COLS), EMPTY, F32)
        ls[g] = jnp.zeros((1, COLS), F32)
        acc[g] = jnp.zeros((HD, COLS), F32)

    pl.semaphore_wait(barrier, len(targets))

    def q_copy(dx, dy):
        yy = lax.rem(y + dy, NY)
        i = dy * NX + dx
        return copy(qown.at[yy], qb.at[y, x], qss.at[i], qrs.at[i], dev(lax.rem(x + dx, NX), yy, z, c))

    def kv_send(zz, yy, send, device):
        part = kv.at[zz, c, yy]
        copy(part, part, send, rs.at[zz, yy], device).start()

    def kv_wait(zz, yy):
        part = kv.at[zz, c, yy]
        copy(part, part, yo.at[0], rs.at[zz, yy], dev(x, y, z, 1 - c)).wait_recv()

    kv_send(z, y, yo.at[0], dev(x, opp, z, c))
    for dx, dy in peers:
        q_copy(dx, dy).start()
    kv_send(z, y, zs.at[0, 0], dev(x, y, zdn, c))
    kv_send(z, y, zs.at[0, 7], dev(x, y, zup, c))
    kv_send(z, y, ys.at[0, 0], dev(x, yup, z, c))
    kv_send(z, y, ys.at[1, 0], dev(x, ydn, z, c))

    def place(n):
        d = lax.div(n + 1, 2)
        return lax.rem(z + NZ + d * (2 * lax.rem(n, 2) - 1), NZ)

    def stage_z(n):
        zz = place(n)
        odd = lax.rem(n, 2)
        nxt = odd * zdn + (1 - odd) * zup
        kv_wait(zz, y)

        @pl.when((n <= 4) | (n == 6))
        def _():
            kv_send(zz, y, zs.at[0, n], dev(x, y, nxt, c))

        kv_send(zz, y, ys.at[0, n], dev(x, yup, z, c))
        kv_send(zz, y, ys.at[1, n], dev(x, ydn, z, c))
        kv_wait(zz, opp)

        @pl.when(n <= 5)
        def _():
            kv_send(zz, opp, zs.at[1, n], dev(x, y, nxt, c))

    def both_copy(n):
        zz = place(n)
        part = kv.at[zz, c]
        return copy(part, part, ss.at[n], sr.at[zz], dev(x, y, z, 1 - c))

    def stage_y(n):
        zz = place(n)
        kv_wait(zz, yup)
        kv_wait(zz, ydn)
        both_copy(n).start()

    def stage_c(n):
        zz = place(n)
        part = kv.at[zz, 1 - c]
        copy(part, part, ss.at[0], sr.at[zz], dev(x, y, z, 1 - c)).wait_recv()

    kv_wait(z, opp)
    kv_send(z, opp, zs.at[1, 0], dev(x, y, zdn, c))
    kv_send(z, opp, zs.at[1, 7], dev(x, y, zup, c))
    stage_y(jnp.int32(0))
    stage_z(jnp.int32(1))
    stage_z(jnp.int32(2))
    stage_y(jnp.int32(1))
    for dx, dy in peers:
        q_copy(dx, dy).wait_recv()
    stage_c(jnp.int32(0))

    apart = lax.broadcasted_iota(jnp.int32, (BLK, COLS), 0) - lax.rem(
        lax.broadcasted_iota(jnp.int32, (BLK, COLS), 1), BLK
    )

    def score(n, g):
        zz = place(n)
        depth = (g + 1) * BLK
        k = kv[zz, :, :g + 1, :BLK, :].reshape(2 * depth, HD)
        q = jnp.concatenate([qb[g, h] for h in range(NX)], axis=1)
        s = jnp.dot(k, q, preferred_element_type=F32)
        parts = []
        for cc in range(2):
            ahead = (zz - z) * 1024 + (cc - c) * 512 + (x - y) * BLK
            last = s[(cc + 1) * depth - BLK:(cc + 1) * depth]
            parts.append(s[cc * depth:(cc + 1) * depth - BLK])
            parts.append(jnp.where(apart <= -ahead, last, HIDDEN))
        s = jnp.concatenate([p for p in parts if p.shape[0]], axis=0)
        scores[g][...] = s
        before = mx[g]
        mp[g] = before
        mx[g] = jnp.maximum(before, jnp.max(s, axis=0, keepdims=True))

    def weigh(n, g, before, now):
        zz = place(n)
        p = jnp.exp2(scores[g][...] * SCALE - now * SCALE)
        v = jnp.concatenate([kv[zz, cc, yy, BLK:, :] for cc in range(2) for yy in range(g + 1)], axis=1)
        old = jnp.exp2((before - now) * SCALE)
        ls[g] = ls[g] * old + jnp.sum(p, axis=0, keepdims=True)
        acc[g] = acc[g] * old + jnp.dot(v, p.astype(BF16), preferred_element_type=F32)

    def step(n, g, m, g_next):
        before, now = mp[g], mx[g]
        score(m, g_next)
        weigh(n, g, before, now)

    score(jnp.int32(0), ORDER[0])

    def unit(n, carry):
        for i in range(NY - 1):
            step(n, ORDER[i], n, ORDER[i + 1])

        @pl.when(n + 3 < NZ)
        def _():
            stage_z(n + 3)

        @pl.when(n + 2 < NZ)
        def _():
            stage_y(n + 2)

        @pl.when(n + 1 < NZ)
        def _():
            stage_c(n + 1)

        step(n, ORDER[NY - 1], jnp.minimum(n + 1, NZ - 1), ORDER[0])
        return carry

    lax.fori_loop(0, NZ, unit, 0)

    line = lax.broadcasted_iota(jnp.int32, (16, BLK), 0)

    def thirds(a):
        high = a.astype(BF16).astype(F32)
        mid = (a - high).astype(BF16).astype(F32)
        return high, mid, a - high - mid

    def finish(g):
        total = acc[g].astype(BF16)
        for h in range(NX):
            lanes = slice(h * BLK, (h + 1) * BLK)
            osend[g, h, :HD, :] = total[:, lanes]
            now, count = mx[g][:, lanes], ls[g][:, lanes]
            side = jnp.zeros((16, BLK), F32)
            for i, part in enumerate(thirds(now) + thirds(count)):
                side = jnp.where(line == i, part, side)
            osend[g, h, HD:, :] = side.astype(BF16)

    def o_copy(dx, dy):
        xx, yy = lax.rem(x + dx, NX), lax.rem(y + dy, NY)
        i = dy * NX + dx
        return copy(osend.at[yy, xx], orecv.at[y, x], oss.at[i], ors.at[i], dev(xx, yy, z, c))

    for g in range(NY):
        finish(g)
    for dx, dy in peers:
        o_copy(dx, dy).start()
    orecv[y, x] = osend[y, x]

    here = dev(x, y, z, 1 - c)
    one = kv.at[z, c, y]
    for n in range(NZ):
        if n != 5:
            copy(one, one, zs.at[0, n], rs.at[z, y], here).wait_send()
        if n != 6:
            copy(one, one, zs.at[1, n], rs.at[z, y], here).wait_send()
        for way in range(2):
            copy(one, one, ys.at[way, n], rs.at[z, y], here).wait_send()
        both_copy(jnp.int32(n)).wait_send()
    copy(one, one, yo.at[0], rs.at[z, y], here).wait_send()
    for dx, dy in peers:
        q_copy(dx, dy).wait_send()

    for dx, dy in peers:
        o_copy(dx, dy).wait_recv()

    def combine(r):
        sides = [orecv[r, h, HD:, :].astype(F32) for h in range(NX)]
        tops = [side[0:1] + side[1:2] + side[2:3] for side in sides]
        counts = [side[3:4] + side[4:5] + side[5:6] for side in sides]
        top = jnp.maximum(jnp.maximum(tops[0], tops[1]), jnp.maximum(tops[2], tops[3]))
        shares = [jnp.exp2((t - top) * SCALE) for t in tops]
        inverse = 1.0 / sum(share * count for share, count in zip(shares, counts))
        total = sum((share * inverse) * orecv[r, h, :HD, :].astype(F32) for h, share in enumerate(shares))
        o_ref[r * BLK:(r + 1) * BLK, :] = total.T.astype(BF16)

    for r in range(NY):
        combine(r)
    for dx, dy in peers:
        o_copy(dx, dy).wait_send()


def body(queries, keys, values):
    vmem = pl.BlockSpec(memory_space=pltpu.VMEM)
    dma = pltpu.SemaphoreType.DMA
    scratch = [
        pltpu.VMEM((NZ, 2, NY, 2 * BLK, HD), BF16),
        pltpu.VMEM((NY, HD, BLK), BF16),
        pltpu.VMEM((NY, NX, HD, BLK), BF16),
    ]
    scratch += [pltpu.VMEM((2 * BLK * (g + 1), COLS), F32) for g in range(NY)]
    scratch += [pltpu.VMEM((NY, 1, COLS), F32) for _ in range(3)]
    scratch += [
        pltpu.VMEM((NY, HD, COLS), F32),
        pltpu.VMEM((NY, NX, HD + 16, BLK), BF16),
        pltpu.VMEM((NY, NX, HD + 16, BLK), BF16),
        dma((NZ, NY)), dma((2, NZ)), dma((2, NZ)), dma((1,)), dma((NZ,)), dma((NZ,)),
        dma((16,)), dma((16,)), dma((16,)), dma((16,)),
    ]
    return pl.pallas_call(
        kernel,
        out_shape=jax.ShapeDtypeStruct(queries.shape, BF16),
        in_specs=[vmem] * 3,
        out_specs=vmem,
        scratch_shapes=scratch,
        compiler_params=pltpu.CompilerParams(
            collective_id=0, has_side_effects=True, vmem_limit_bytes=40 * 1024 * 1024
        ),
    )(queries, keys, values)


def solution(mesh):
    placed = (P("ctx", "head"), P("ctx", None), P("ctx", None))
    return jax.shard_map(
        body, mesh=mesh, in_specs=placed, out_specs=P("ctx", "head"), check_vma=False
    )
```

```python
import math

import jax
import jax.numpy as jnp
from jax import lax
from jax.experimental import pallas as pl
from jax.experimental.pallas import tpu as pltpu
from jax.sharding import PartitionSpec as P

MESH = pl.DeviceIdType.MESH
NX, NY, NZ = 4, 4, 8
BLK = 128
HD = 128
COLS = 512
SCALE = math.log2(math.e) / math.sqrt(HD)
EMPTY = -1e30
HIDDEN = -2e30
WAYS = (2, 1, 3)
F32 = jnp.float32
BF16 = jnp.bfloat16


def kernel(
    q_hbm, k_hbm, v_hbm, o_ref,
    q_ref, k_ref, v_ref, kv, qb, s0, s1, s2, s3, mx, mp, ls, acc, osend, orecv,
    ins, rs, zs, ys, yo, ss, sr, qss, qrs, oss, ors,
):
    scores = (s0, s1, s2, s3)
    ctx, x = lax.axis_index("ctx"), lax.axis_index("head")
    c = lax.rem(ctx, 2)
    z = lax.rem(lax.div(ctx, 2), NZ)
    y = lax.div(ctx, 2 * NZ)
    opp = lax.rem(y + 2, NY)
    yup, ydn = lax.rem(y + 1, NY), lax.rem(y + NY - 1, NY)
    zup, zdn = lax.rem(z + 1, NZ), lax.rem(z + NZ - 1, NZ)

    def dev(xx, yy, zz, cc):
        return ((yy * NZ + zz) * 2 + cc, xx)

    def copy(src, dst, send, recv, device):
        return pltpu.make_async_remote_copy(
            src_ref=src, dst_ref=dst, send_sem=send, recv_sem=recv, device_id=device, device_id_type=MESH
        )

    rows = pl.ds(pl.multiple_of(x * BLK, BLK), BLK)
    loads = [
        pltpu.make_async_copy(q_hbm, q_ref, ins.at[0]),
        pltpu.make_async_copy(k_hbm.at[rows], k_ref, ins.at[1]),
        pltpu.make_async_copy(v_hbm.at[rows], v_ref, ins.at[2]),
    ]
    for load in loads:
        load.start()
    barrier = pltpu.get_barrier_semaphore()
    targets = [dev(lax.rem(x + dx, NX), y, z, c) for dx in WAYS]
    targets += [dev(x, yy, z, c) for yy in (opp, yup, ydn)]
    targets += [dev(x, y, zup, c), dev(x, y, zdn, c), dev(x, y, z, 1 - c)]
    for target in targets:
        pl.semaphore_signal(barrier, inc=1, device_id=target, device_id_type=MESH)

    def turn(a):
        return a.astype(F32).T.astype(BF16)

    for g in range(NY):
        mx[g] = jnp.full((1, COLS), EMPTY, F32)
        ls[g] = jnp.zeros((1, COLS), F32)
        acc[g] = jnp.zeros((HD, COLS), F32)
    loads[0].wait()
    qb[x] = turn(q_ref[...])
    loads[1].wait()
    kv[z, c, y, :BLK, :] = k_ref[...]
    loads[2].wait()
    kv[z, c, y, BLK:, :] = turn(v_ref[...])

    pl.semaphore_wait(barrier, len(targets))

    def q_copy(dx):
        part = qb.at[x]
        return copy(part, part, qss.at[dx], qrs.at[dx], dev(lax.rem(x + dx, NX), y, z, c))

    def kv_send(zz, yy, send, device):
        part = kv.at[zz, c, yy]
        copy(part, part, send, rs.at[zz, yy], device).start()

    def kv_wait(zz, yy):
        part = kv.at[zz, c, yy]
        copy(part, part, yo.at[0], rs.at[zz, yy], dev(x, y, z, 1 - c)).wait_recv()

    kv_send(z, y, yo.at[0], dev(x, opp, z, c))
    kv_send(z, y, zs.at[0, 0], dev(x, y, zdn, c))
    kv_send(z, y, zs.at[0, 7], dev(x, y, zup, c))
    kv_send(z, y, ys.at[0, 0], dev(x, yup, z, c))
    kv_send(z, y, ys.at[1, 0], dev(x, ydn, z, c))
    for dx in (1, 3, 2):
        q_copy(dx).start()

    def place(n):
        d = lax.div(n + 1, 2) if not isinstance(n, int) else (n + 1) // 2
        side = 2 * (n % 2 if isinstance(n, int) else lax.rem(n, 2)) - 1
        return lax.rem(z + NZ + d * side, NZ)

    def onward(n):
        odd = n % 2 if isinstance(n, int) else lax.rem(n, 2)
        return dev(x, y, odd * zdn + (1 - odd) * zup, c)

    def stage_own(n):
        zz = place(n)
        kv_wait(zz, y)
        if n in (1, 2, 3, 4, 6):
            kv_send(zz, y, zs.at[0, n], onward(n))
        kv_send(zz, y, ys.at[0, n], dev(x, yup, z, c))
        kv_send(zz, y, ys.at[1, n], dev(x, ydn, z, c))

    def stage_opp(n):
        zz = place(n)
        kv_wait(zz, opp)
        if isinstance(n, int):
            if n <= 5:
                kv_send(zz, opp, zs.at[1, n], onward(n))
        else:

            @pl.when(n <= 5)
            def _():
                kv_send(zz, opp, zs.at[1, n], onward(n))

    def both_copy(n):
        zz = place(n)
        part = kv.at[zz, c]
        return copy(part, part, ss.at[n], sr.at[zz], dev(x, y, z, 1 - c))

    def stage_y(n):
        zz = place(n)
        kv_wait(zz, yup)
        kv_wait(zz, ydn)
        both_copy(n).start()

    def stage_c(n):
        zz = place(n)
        part = kv.at[zz, 1 - c]
        copy(part, part, ss.at[0], sr.at[zz], dev(x, y, z, 1 - c)).wait_recv()

    stage_own(1)
    stage_own(2)
    kv_wait(z, opp)
    kv_send(z, opp, zs.at[1, 0], dev(x, y, zdn, c))
    kv_send(z, opp, zs.at[1, 7], dev(x, y, zup, c))
    stage_y(0)
    stage_own(3)
    stage_own(4)
    stage_c(0)

    apart = lax.broadcasted_iota(jnp.int32, (BLK, COLS), 0) - lax.broadcasted_iota(jnp.int32, (BLK, COLS), 1)

    def slab(back):
        return lax.rem(y + NY - back, NY)

    def score(n, dx, to):
        zz, h = place(n), lax.rem(x + dx, NX)
        k = jnp.concatenate([kv[zz, :, slab(back), :BLK, :].reshape(2 * BLK, HD) for back in range(NY)], axis=0)
        s = jnp.dot(k, qb[h], preferred_element_type=F32)
        parts = []
        for cc in range(2):
            ahead = (zz - z) * 1024 + (cc - c) * 512 + x * BLK
            parts.append(jnp.where(apart <= -ahead, s[cc * BLK:(cc + 1) * BLK], HIDDEN))
        for back in range(1, NY):
            parts.append(jnp.where(back <= y, s[2 * back * BLK:2 * (back + 1) * BLK], HIDDEN))
        s = jnp.concatenate(parts, axis=0)
        to[...] = s
        before = mx[dx]
        mp[dx] = before
        mx[dx] = jnp.maximum(before, jnp.max(s, axis=0, keepdims=True))

    def weigh(n, dx, at, before, now):
        zz = place(n)
        old = jnp.exp2((before - now) * SCALE)
        p = jnp.exp2(at[...] * SCALE - now * SCALE)
        v = jnp.concatenate([kv[zz, cc, slab(back), BLK:, :] for back in range(NY) for cc in range(2)], axis=1)
        ls[dx] = ls[dx] * old + jnp.sum(p, axis=0, keepdims=True)
        acc[dx] = acc[dx] * old + jnp.dot(v, p.astype(BF16), preferred_element_type=F32)

    line = lax.broadcasted_iota(jnp.int32, (16, COLS), 0)

    def thirds(a):
        high = a.astype(BF16).astype(F32)
        mid = (a - high).astype(BF16).astype(F32)
        return high, mid, a - high - mid

    def finish(dx):
        osend[dx, :HD, :] = acc[dx].astype(BF16)
        side = jnp.zeros((16, COLS), F32)
        for i, part in enumerate(thirds(mx[dx]) + thirds(ls[dx])):
            side = jnp.where(line == i, part, side)
        osend[dx, HD:, :] = side.astype(BF16)

    def o_copy(dx):
        h = lax.rem(x + dx, NX)
        return copy(osend.at[dx], orecv.at[dx], oss.at[dx], ors.at[dx], dev(h, y, z, c))

    def combine():
        held = [(osend if dx == 0 else orecv).at[dx] for dx in range(NX)]
        sides = [part[HD:, :].astype(F32) for part in held]
        tops = [side[0:1] + side[1:2] + side[2:3] for side in sides]
        counts = [side[3:4] + side[4:5] + side[5:6] for side in sides]
        top = jnp.maximum(jnp.maximum(tops[0], tops[1]), jnp.maximum(tops[2], tops[3]))
        shares = [jnp.exp2((t - top) * SCALE) for t in tops]
        inverse = 1.0 / sum(share * count for share, count in zip(shares, counts))
        total = sum((share * inverse) * part[:HD, :].astype(F32) for part, share in zip(held, shares))
        o_ref[...] = total.T.astype(BF16)

    def step(n, dx, at, n_next, dx_next, to):
        before, now = mp[dx], mx[dx]
        score(n_next, dx_next, to)
        weigh(n, dx, at, before, now)

    def q_wait(dx):
        q_copy(NX - dx).wait_recv()

    score(0, 0, s0)
    q_wait(1)
    step(0, 0, s0, 0, 1, s1)
    q_wait(3)
    step(0, 1, s1, 0, 3, s2)
    stage_opp(1)
    stage_opp(2)
    stage_y(1)
    stage_y(2)
    q_wait(2)
    step(0, 3, s2, 0, 2, s3)
    stage_own(5)
    stage_own(6)
    stage_c(1)
    step(0, 2, s3, 1, 0, s0)
    step(1, 0, s0, 1, 1, s1)
    step(1, 1, s1, 1, 3, s2)
    stage_opp(3)
    stage_opp(4)
    stage_y(3)
    stage_y(4)
    step(1, 3, s2, 1, 2, s3)
    stage_c(2)
    step(1, 2, s3, 2, 2, s0)

    def unit(n, carry):
        step(n, 2, s0, n, 1, s1)

        @pl.when(n == 2)
        def _():
            stage_own(7)

        @pl.when((n == 3) | (n == 4))
        def _():
            stage_opp(n + 2)
            stage_y(n + 2)

        step(n, 1, s1, n, 3, s2)

        @pl.when(n == 5)
        def _():
            stage_opp(7)
            stage_y(7)

        stage_c(n + 1)
        step(n, 3, s2, n + 1, 2, s0)
        return carry

    lax.fori_loop(2, 6, unit, 0)

    tail = [(n, dx) for dx in WAYS for n in (6, 7)] + [(n, 0) for n in range(2, NZ)]
    at, to = s0, s1
    for i, (n, dx) in enumerate(tail):
        if i == 0:
            stage_c(7)
        if i + 1 < len(tail):
            step(n, dx, at, *tail[i + 1], to)
            at, to = to, at
        else:
            weigh(n, dx, at, mp[dx], mx[dx])
        if n == NZ - 1:
            finish(dx)
            if dx:
                o_copy(dx).start()
    for dx in WAYS:
        o_copy(dx).wait_recv()
    combine()

    here = dev(x, y, z, 1 - c)
    one = kv.at[z, c, y]
    for n in range(NZ):
        if n != 5:
            copy(one, one, zs.at[0, n], rs.at[z, y], here).wait_send()
        if n != 6:
            copy(one, one, zs.at[1, n], rs.at[z, y], here).wait_send()
        for way in range(2):
            copy(one, one, ys.at[way, n], rs.at[z, y], here).wait_send()
        both_copy(n).wait_send()
    copy(one, one, yo.at[0], rs.at[z, y], here).wait_send()
    for dx in WAYS:
        q_copy(dx).wait_send()

    for dx in WAYS:
        o_copy(dx).wait_send()


def body(queries, keys, values):
    dma = pltpu.SemaphoreType.DMA
    scratch = [
        pltpu.VMEM(queries.shape, BF16),
        pltpu.VMEM((BLK, HD), BF16),
        pltpu.VMEM((BLK, HD), BF16),
        pltpu.VMEM((NZ, 2, NY, 2 * BLK, HD), BF16),
        pltpu.VMEM((NX, HD, COLS), BF16),
    ]
    scratch += [pltpu.VMEM((2 * BLK * NY, COLS), F32) for _ in range(4)]
    scratch += [pltpu.VMEM((NY, 1, COLS), F32) for _ in range(3)]
    scratch += [
        pltpu.VMEM((NX, HD, COLS), F32),
        pltpu.VMEM((NX, HD + 16, COLS), BF16),
        pltpu.VMEM((NX, HD + 16, COLS), BF16),
        dma((3,)), dma((NZ, NY)), dma((2, NZ)), dma((2, NZ)), dma((1,)), dma((NZ,)), dma((NZ,)),
        dma((NX,)), dma((NX,)), dma((NX,)), dma((NX,)),
    ]
    return pl.pallas_call(
        kernel,
        out_shape=jax.ShapeDtypeStruct(queries.shape, BF16),
        in_specs=[pl.BlockSpec(memory_space=pltpu.HBM)] * 3,
        out_specs=pl.BlockSpec(memory_space=pltpu.VMEM),
        scratch_shapes=scratch,
        compiler_params=pltpu.CompilerParams(
            collective_id=0, has_side_effects=True, vmem_limit_bytes=62 * 1024 * 1024
        ),
    )(queries, keys, values)


def solution(mesh):
    placed = (P("ctx", "head"), P("ctx", None), P("ctx", None))
    return jax.shard_map(
        body, mesh=mesh, in_specs=placed, out_specs=P("ctx", "head"), check_vma=False
    )
```

```python
import math

import jax
import jax.numpy as jnp
from jax import lax
from jax.experimental import pallas as pl
from jax.experimental.pallas import tpu as pltpu
from jax.sharding import PartitionSpec as P

MESH = pl.DeviceIdType.MESH
NX, NY, NZ = 4, 4, 8
BLK = 128
HD = 128
COLS = 512
SCALE = math.log2(math.e) / math.sqrt(HD)
EMPTY = -1e30
HIDDEN = -2e30
WAYS = (2, 1, 3)
RING = {0: (1, 2), 1: (3,), 2: (4,), 3: (5,), 4: (6,)}
OWN_WAY = {**RING, 6: (7,)}
OPP_WAY = {**RING, 5: (7,)}
F32 = jnp.float32
BF16 = jnp.bfloat16


def kernel(
    q_hbm, k_hbm, v_hbm, o_ref,
    q_ref, k_ref, v_ref, kv, qb, s0, s1, s2, s3, mx, mp, ls, acc, osend, orecv,
    ins, rs, zs, ys, yo, ss, sr, qss, qrs, oss, ors,
):
    scores = (s0, s1, s2, s3)
    ctx, x = lax.axis_index("ctx"), lax.axis_index("head")
    c = lax.rem(ctx, 2)
    z = lax.rem(lax.div(ctx, 2), NZ)
    y = lax.div(ctx, 2 * NZ)
    opp = lax.rem(y + 2, NY)
    yup, ydn = lax.rem(y + 1, NY), lax.rem(y + NY - 1, NY)

    def dev(xx, yy, zz, cc):
        return ((yy * NZ + zz) * 2 + cc, xx)

    def copy(src, dst, send, recv, device):
        return pltpu.make_async_remote_copy(
            src_ref=src, dst_ref=dst, send_sem=send, recv_sem=recv, device_id=device, device_id_type=MESH
        )

    rows = pl.ds(pl.multiple_of(x * BLK, BLK), BLK)
    loads = [
        pltpu.make_async_copy(q_hbm, q_ref, ins.at[0]),
        pltpu.make_async_copy(k_hbm.at[rows], k_ref, ins.at[1]),
        pltpu.make_async_copy(v_hbm.at[rows], v_ref, ins.at[2]),
    ]
    for load in loads:
        load.start()
    barrier = pltpu.get_barrier_semaphore()
    targets = [dev(lax.rem(x + dx, NX), y, z, c) for dx in WAYS]
    targets += [dev(x, yy, z, c) for yy in (opp, yup, ydn)]
    targets += [dev(x, y, lax.rem(z + d, NZ), c) for d in (1, NZ - 1)] + [dev(x, y, z, 1 - c)]
    for target in targets:
        pl.semaphore_signal(barrier, inc=1, device_id=target, device_id_type=MESH)

    def turn(a):
        return a.astype(F32).T.astype(BF16)

    for g in range(NY):
        mx[g] = jnp.full((1, COLS), EMPTY, F32)
        ls[g] = jnp.zeros((1, COLS), F32)
        acc[g] = jnp.zeros((HD, COLS), F32)
    for yy in range(1, NY):

        @pl.when(yy > y)
        def _():
            for zz in range(NZ):
                kv[zz, c, yy] = jnp.zeros((2 * BLK, HD), BF16)

    loads[0].wait()
    qb[x] = turn(q_ref[...])
    loads[1].wait()
    kv[z, c, y, :BLK, :] = k_ref[...]
    loads[2].wait()
    kv[z, c, y, BLK:, :] = turn(v_ref[...])

    pl.semaphore_wait(barrier, len(targets))

    def q_copy(dx):
        part = qb.at[x]
        return copy(part, part, qss.at[dx], qrs.at[dx], dev(lax.rem(x + dx, NX), y, z, c))

    def kv_send(zz, yy, send, device):
        part = kv.at[zz, c, yy]
        copy(part, part, send, rs.at[zz, yy], device).start()

    def kv_wait(zz, yy):
        part = kv.at[zz, c, yy]
        copy(part, part, yo.at[0], rs.at[zz, yy], dev(x, y, z, 1 - c)).wait_recv()

    def shift(n):
        d, odd = (n + 1) // 2, n % 2
        return d * (2 * odd - 1)

    def place(n):
        if not isinstance(n, int):
            return lax.rem(z + NZ + lax.div(n + 1, 2) * (2 * lax.rem(n, 2) - 1), NZ)
        return lax.rem(z + NZ + shift(n), NZ)

    def kv_along(item, n):
        zz = place(n)
        for m in (OWN_WAY, OPP_WAY)[item].get(n, ()):
            kv_send(zz, (y, opp)[item], zs.at[item, m], dev(x, y, lax.rem(zz + NZ - shift(m), NZ), c))

    def send_y(n):
        zz = place(n)

        @pl.when(y < NY - 1)
        def _():
            kv_send(zz, y, ys.at[0, n], dev(x, yup, z, c))

        @pl.when(y == 0)
        def _():
            kv_send(zz, y, ys.at[1, n], dev(x, ydn, z, c))

    def stage_own(n):
        zz = place(n)
        kv_wait(zz, y)
        kv_along(0, n)
        send_y(n)

    def stage_opp(n):
        @pl.when(y >= 2)
        def _():
            kv_wait(place(n), opp)
            kv_along(1, n)


    @pl.when(y < 2)
    def _():
        kv_send(z, y, yo.at[0], dev(x, opp, z, c))

    kv_along(0, 0)
    send_y(0)
    for dx in (1, 3, 2):
        q_copy(dx).start()

    def both_copy(n):
        zz = place(n)
        part = kv.at[zz, c]
        return copy(part, part, ss.at[n], sr.at[zz], dev(x, y, z, 1 - c))

    def stage_y(n):
        zz = place(n)

        @pl.when(y == NY - 1)
        def _():
            kv_wait(zz, yup)

        @pl.when(y > 0)
        def _():
            kv_wait(zz, ydn)

        both_copy(n).start()

    def stage_c(n):
        zz = place(n)
        part = kv.at[zz, 1 - c]
        copy(part, part, ss.at[0], sr.at[zz], dev(x, y, z, 1 - c)).wait_recv()

    stage_own(1)
    stage_own(2)
    stage_opp(0)
    stage_y(0)
    stage_c(0)

    apart = lax.broadcasted_iota(jnp.int32, (BLK, COLS), 0) - lax.broadcasted_iota(jnp.int32, (BLK, COLS), 1)

    def slab(back):
        return lax.rem(y + NY - back, NY)

    def score(n, dx, to):
        zz, h = place(n), lax.rem(x + dx, NX)
        k = jnp.concatenate([kv[zz, :, slab(back), :BLK, :].reshape(2 * BLK, HD) for back in range(NY)], axis=0)
        s = jnp.dot(k, qb[h], preferred_element_type=F32)
        parts = []
        for cc in range(2):
            ahead = (zz - z) * 1024 + (cc - c) * 512 + x * BLK
            parts.append(jnp.where(apart <= -ahead, s[cc * BLK:(cc + 1) * BLK], HIDDEN))
        for back in range(1, NY):
            parts.append(jnp.where(back <= y, s[2 * back * BLK:2 * (back + 1) * BLK], HIDDEN))
        s = jnp.concatenate(parts, axis=0)
        to[...] = s
        before = mx[dx]
        mp[dx] = before
        mx[dx] = jnp.maximum(before, jnp.max(s, axis=0, keepdims=True))

    def weigh(n, dx, at, before, now):
        zz = place(n)
        old = jnp.exp2((before - now) * SCALE)
        p = jnp.exp2(at[...] * SCALE - now * SCALE)
        v = jnp.concatenate([kv[zz, cc, slab(back), BLK:, :] for back in range(NY) for cc in range(2)], axis=1)
        ls[dx] = ls[dx] * old + jnp.sum(p, axis=0, keepdims=True)
        acc[dx] = acc[dx] * old + jnp.dot(v, p.astype(BF16), preferred_element_type=F32)

    line = lax.broadcasted_iota(jnp.int32, (16, COLS), 0)

    def thirds(a):
        high = a.astype(BF16).astype(F32)
        mid = (a - high).astype(BF16).astype(F32)
        return high, mid, a - high - mid

    def finish(dx):
        osend[dx, :HD, :] = acc[dx].astype(BF16)
        side = jnp.zeros((16, COLS), F32)
        for i, part in enumerate(thirds(mx[dx]) + thirds(ls[dx])):
            side = jnp.where(line == i, part, side)
        osend[dx, HD:, :] = side.astype(BF16)

    def o_copy(dx):
        h = lax.rem(x + dx, NX)
        return copy(osend.at[dx], orecv.at[dx], oss.at[dx], ors.at[dx], dev(h, y, z, c))

    def combine():
        held = [(osend if dx == 0 else orecv).at[dx] for dx in range(NX)]
        sides = [part[HD:, :].astype(F32) for part in held]
        tops = [side[0:1] + side[1:2] + side[2:3] for side in sides]
        counts = [side[3:4] + side[4:5] + side[5:6] for side in sides]
        top = jnp.maximum(jnp.maximum(tops[0], tops[1]), jnp.maximum(tops[2], tops[3]))
        shares = [jnp.exp2((t - top) * SCALE) for t in tops]
        inverse = 1.0 / sum(share * count for share, count in zip(shares, counts))
        total = sum((share * inverse) * part[:HD, :].astype(F32) for part, share in zip(held, shares))
        o_ref[...] = total.T.astype(BF16)

    def step(n, dx, at, n_next, dx_next, to):
        before, now = mp[dx], mx[dx]
        score(n_next, dx_next, to)
        weigh(n, dx, at, before, now)

    def q_wait(dx):
        q_copy(NX - dx).wait_recv()

    score(0, 0, s0)
    q_wait(1)
    step(0, 0, s0, 0, 1, s1)
    stage_own(3)
    stage_own(4)
    q_wait(3)
    step(0, 1, s1, 0, 3, s2)
    stage_opp(1)
    stage_opp(2)
    stage_y(1)
    stage_y(2)
    q_wait(2)
    step(0, 3, s2, 0, 2, s3)
    stage_c(1)
    step(0, 2, s3, 1, 0, s0)
    stage_own(5)
    stage_own(6)
    step(1, 0, s0, 1, 1, s1)
    step(1, 1, s1, 1, 3, s2)
    stage_opp(3)
    stage_opp(4)
    stage_y(3)
    stage_y(4)
    step(1, 3, s2, 1, 2, s3)
    stage_c(2)
    step(1, 2, s3, 2, 2, s0)

    def unit(n, carry):
        step(n, 2, s0, n, 1, s1)

        @pl.when(n == 2)
        def _():
            stage_own(7)

        for m in (5, 6):

            @pl.when(n == m - 2)
            def _():
                stage_opp(m)
                stage_y(m)

        step(n, 1, s1, n, 3, s2)

        @pl.when(n == 5)
        def _():
            stage_opp(7)
            stage_y(7)

        stage_c(n + 1)
        step(n, 3, s2, n + 1, 2, s0)
        return carry

    lax.fori_loop(2, 6, unit, 0)

    tail = [(n, dx) for dx in WAYS for n in (6, 7)] + [(n, 0) for n in range(2, NZ)]
    at, to = s0, s1
    for i, (n, dx) in enumerate(tail):
        if i == 0:
            stage_c(7)
        if i + 1 < len(tail):
            step(n, dx, at, *tail[i + 1], to)
            at, to = to, at
        else:
            weigh(n, dx, at, mp[dx], mx[dx])
        if n == NZ - 1:
            finish(dx)
            if dx:
                o_copy(dx).start()
    here = dev(x, y, z, 1 - c)
    one = kv.at[z, c, y]

    def sent(send):
        copy(one, one, send, rs.at[z, y], here).wait_send()

    for n in range(1, NZ):
        sent(zs.at[0, n])
    for n in range(NZ):
        both_copy(n).wait_send()

    @pl.when(y >= 2)
    def _():
        for n in range(1, NZ):
            sent(zs.at[1, n])

    @pl.when(y < 2)
    def _():
        sent(yo.at[0])

    @pl.when(y < NY - 1)
    def _():
        for n in range(NZ):
            sent(ys.at[0, n])

    @pl.when(y == 0)
    def _():
        for n in range(NZ):
            sent(ys.at[1, n])

    for dx in WAYS:
        q_copy(dx).wait_send()

    for dx in WAYS:
        o_copy(dx).wait_recv()
    combine()

    for dx in WAYS:
        o_copy(dx).wait_send()


def body(queries, keys, values):
    dma = pltpu.SemaphoreType.DMA
    scratch = [
        pltpu.VMEM(queries.shape, BF16),
        pltpu.VMEM((BLK, HD), BF16),
        pltpu.VMEM((BLK, HD), BF16),
        pltpu.VMEM((NZ, 2, NY, 2 * BLK, HD), BF16),
        pltpu.VMEM((NX, HD, COLS), BF16),
    ]
    scratch += [pltpu.VMEM((2 * BLK * NY, COLS), F32) for _ in range(4)]
    scratch += [pltpu.VMEM((NY, 1, COLS), F32) for _ in range(3)]
    scratch += [
        pltpu.VMEM((NX, HD, COLS), F32),
        pltpu.VMEM((NX, HD + 16, COLS), BF16),
        pltpu.VMEM((NX, HD + 16, COLS), BF16),
        dma((3,)), dma((NZ, NY)), dma((2, NZ)), dma((2, NZ)), dma((1,)), dma((NZ,)), dma((NZ,)),
        dma((NX,)), dma((NX,)), dma((NX,)), dma((NX,)),
    ]
    return pl.pallas_call(
        kernel,
        out_shape=jax.ShapeDtypeStruct(queries.shape, BF16),
        in_specs=[pl.BlockSpec(memory_space=pltpu.HBM)] * 3,
        out_specs=pl.BlockSpec(memory_space=pltpu.VMEM),
        scratch_shapes=scratch,
        compiler_params=pltpu.CompilerParams(
            collective_id=0, has_side_effects=True, vmem_limit_bytes=62 * 1024 * 1024
        ),
    )(queries, keys, values)


def solution(mesh):
    placed = (P("ctx", "head"), P("ctx", None), P("ctx", None))
    return jax.shard_map(
        body, mesh=mesh, in_specs=placed, out_specs=P("ctx", "head"), check_vma=False
    )
```

```python
import math

import jax
import jax.numpy as jnp
from jax import lax
from jax.experimental import pallas as pl
from jax.experimental.pallas import tpu as pltpu
from jax.sharding import PartitionSpec as P

MESH = pl.DeviceIdType.MESH
NX, NY, NZ = 4, 4, 8
BLK = 128
HD = 128
COLS = 512
SCALE = math.log2(math.e) / math.sqrt(HD)
EMPTY = -1e30
HIDDEN = -2e30
WAYS = (2, 1, 3)
RING = {0: (1, 2), 1: (3,), 2: (4,), 3: (5,), 4: (6,)}
OWN_WAY = {**RING, 6: (7,)}
OPP_WAY = {**RING, 5: (7,)}
F32 = jnp.float32
BF16 = jnp.bfloat16


def kernel(
    q_hbm, k_hbm, v_hbm, o_ref,
    q_ref, k_ref, v_ref, kv, qb, s0, s1, s2, s3, mx, mp, ls, acc, osend, orecv,
    ins, rs, zs, ys, yo, ss, sr, qss, qrs, oss, ors,
):
    scores = (s0, s1, s2, s3)
    ctx, x = lax.axis_index("ctx"), lax.axis_index("head")
    c = lax.rem(ctx, 2)
    z = lax.rem(lax.div(ctx, 2), NZ)
    y = lax.div(ctx, 2 * NZ)
    opp = lax.rem(y + 2, NY)
    yup, ydn = lax.rem(y + 1, NY), lax.rem(y + NY - 1, NY)

    def dev(xx, yy, zz, cc):
        return ((yy * NZ + zz) * 2 + cc, xx)

    def copy(src, dst, send, recv, device):
        return pltpu.make_async_remote_copy(
            src_ref=src, dst_ref=dst, send_sem=send, recv_sem=recv, device_id=device, device_id_type=MESH
        )

    rows = pl.ds(pl.multiple_of(x * BLK, BLK), BLK)
    loads = [
        pltpu.make_async_copy(q_hbm, q_ref, ins.at[0]),
        pltpu.make_async_copy(k_hbm.at[rows], k_ref, ins.at[1]),
        pltpu.make_async_copy(v_hbm.at[rows], v_ref, ins.at[2]),
    ]
    for load in loads:
        load.start()
    barrier = pltpu.get_barrier_semaphore()
    targets = [dev(lax.rem(x + dx, NX), y, z, c) for dx in WAYS]
    targets += [dev(x, yy, z, c) for yy in (opp, yup, ydn)]
    targets += [dev(x, y, lax.rem(z + d, NZ), c) for d in (1, NZ - 1)] + [dev(x, y, z, 1 - c)]
    for target in targets:
        pl.semaphore_signal(barrier, inc=1, device_id=target, device_id_type=MESH)

    def turn(a):
        return a.astype(F32).T.astype(BF16)

    for g in range(NY):
        mx[g] = jnp.full((1, COLS), EMPTY, F32)
        ls[g] = jnp.zeros((1, COLS), F32)
        acc[g] = jnp.zeros((HD, COLS), F32)
    for yy in range(1, NY):

        @pl.when(yy > y)
        def _():
            for zz in range(NZ):
                kv[zz, c, yy] = jnp.zeros((2 * BLK, HD), BF16)

    loads[0].wait()
    qb[x] = turn(q_ref[...])
    loads[1].wait()
    kv[z, c, y, :BLK, :] = k_ref[...]
    loads[2].wait()
    kv[z, c, y, BLK:, :] = turn(v_ref[...])

    pl.semaphore_wait(barrier, len(targets))

    def q_copy(dx):
        part = qb.at[x]
        return copy(part, part, qss.at[dx], qrs.at[dx], dev(lax.rem(x + dx, NX), y, z, c))

    def kv_send(zz, yy, send, device):
        part = kv.at[zz, c, yy]
        copy(part, part, send, rs.at[zz, yy], device).start()

    def kv_wait(zz, yy):
        part = kv.at[zz, c, yy]
        copy(part, part, yo.at[0], rs.at[zz, yy], dev(x, y, z, 1 - c)).wait_recv()

    def shift(n):
        d, odd = (n + 1) // 2, n % 2
        return d * (2 * odd - 1)

    def place(n):
        if not isinstance(n, int):
            return lax.rem(z + NZ + lax.div(n + 1, 2) * (2 * lax.rem(n, 2) - 1), NZ)
        return lax.rem(z + NZ + shift(n), NZ)

    def kv_along(item, n):
        zz = place(n)
        for m in (OWN_WAY, OPP_WAY)[item].get(n, ()):
            kv_send(zz, (y, opp)[item], zs.at[item, m], dev(x, y, lax.rem(zz + NZ - shift(m), NZ), c))

    def send_y(n):
        zz = place(n)

        @pl.when(y < NY - 1)
        def _():
            kv_send(zz, y, ys.at[0, n], dev(x, yup, z, c))

        @pl.when(y == 0)
        def _():
            kv_send(zz, y, ys.at[1, n], dev(x, ydn, z, c))

    def stage_own(n):
        zz = place(n)
        kv_wait(zz, y)
        kv_along(0, n)
        send_y(n)

    def stage_opp(n):
        @pl.when(y >= 2)
        def _():
            kv_wait(place(n), opp)
            kv_along(1, n)


    @pl.when(y < 2)
    def _():
        kv_send(z, y, yo.at[0], dev(x, opp, z, c))

    kv_along(0, 0)
    send_y(0)
    for dx in (1, 3, 2):
        q_copy(dx).start()

    def both_copy(n):
        zz = place(n)
        part = kv.at[zz, c]
        return copy(part, part, ss.at[n], sr.at[zz], dev(x, y, z, 1 - c))

    def stage_y(n):
        zz = place(n)

        @pl.when(y == NY - 1)
        def _():
            kv_wait(zz, yup)

        @pl.when(y > 0)
        def _():
            kv_wait(zz, ydn)

        both_copy(n).start()

    def stage_c(n):
        zz = place(n)
        part = kv.at[zz, 1 - c]
        copy(part, part, ss.at[0], sr.at[zz], dev(x, y, z, 1 - c)).wait_recv()

    stage_own(1)
    stage_own(2)
    stage_opp(0)
    stage_y(0)
    stage_c(0)

    apart = lax.broadcasted_iota(jnp.int32, (BLK, COLS), 0) - lax.broadcasted_iota(jnp.int32, (BLK, COLS), 1)

    def slab(back):
        return lax.rem(y + NY - back, NY)

    def score(n, dx, to):
        zz, h = place(n), lax.rem(x + dx, NX)
        k = jnp.concatenate([kv[zz, :, slab(back), :BLK, :].reshape(2 * BLK, HD) for back in range(NY)], axis=0)
        s = jnp.dot(k, qb[h], preferred_element_type=F32)
        own = []
        for cc in range(2):
            ahead = (zz - z) * 1024 + (cc - c) * 512 + x * BLK
            own.append(jnp.where(apart <= -ahead, s[cc * BLK:(cc + 1) * BLK], HIDDEN))
        own = jnp.concatenate(own, axis=0)
        to[:2 * BLK] = own
        to[2 * BLK:] = s[2 * BLK:]
        before = mx[dx]
        mp[dx] = before
        top = jnp.maximum(before, jnp.max(own, axis=0, keepdims=True))
        for back in range(1, NY):
            one = jnp.max(s[2 * back * BLK:2 * (back + 1) * BLK], axis=0, keepdims=True)
            top = jnp.maximum(top, jnp.where(back <= y, one, HIDDEN))
        mx[dx] = top

    def weigh(n, dx, at, before, now):
        zz = place(n)
        old = jnp.exp2((before - now) * SCALE)
        now = now * SCALE
        parts = []
        for back in range(NY):
            row = jnp.where(back <= y, now, -HIDDEN) if back else now
            parts.append(jnp.exp2(at[2 * back * BLK:2 * (back + 1) * BLK] * SCALE - row))
        p = jnp.concatenate(parts, axis=0)
        v = jnp.concatenate([kv[zz, cc, slab(back), BLK:, :] for back in range(NY) for cc in range(2)], axis=1)
        ls[dx] = ls[dx] * old + jnp.sum(p, axis=0, keepdims=True)
        acc[dx] = acc[dx] * old + jnp.dot(v, p.astype(BF16), preferred_element_type=F32)

    line = lax.broadcasted_iota(jnp.int32, (16, COLS), 0)

    def thirds(a):
        high = a.astype(BF16).astype(F32)
        mid = (a - high).astype(BF16).astype(F32)
        return high, mid, a - high - mid

    def finish(dx):
        osend[dx, :HD, :] = acc[dx].astype(BF16)
        side = jnp.zeros((16, COLS), F32)
        for i, part in enumerate(thirds(mx[dx]) + thirds(ls[dx])):
            side = jnp.where(line == i, part, side)
        osend[dx, HD:, :] = side.astype(BF16)

    def o_copy(dx):
        h = lax.rem(x + dx, NX)
        return copy(osend.at[dx], orecv.at[dx], oss.at[dx], ors.at[dx], dev(h, y, z, c))

    def combine():
        held = [(osend if dx == 0 else orecv).at[dx] for dx in range(NX)]
        sides = [part[HD:, :].astype(F32) for part in held]
        tops = [side[0:1] + side[1:2] + side[2:3] for side in sides]
        counts = [side[3:4] + side[4:5] + side[5:6] for side in sides]
        top = jnp.maximum(jnp.maximum(tops[0], tops[1]), jnp.maximum(tops[2], tops[3]))
        shares = [jnp.exp2((t - top) * SCALE) for t in tops]
        inverse = 1.0 / sum(share * count for share, count in zip(shares, counts))
        total = sum((share * inverse) * part[:HD, :].astype(F32) for part, share in zip(held, shares))
        o_ref[...] = total.T.astype(BF16)

    def step(n, dx, at, n_next, dx_next, to):
        before, now = mp[dx], mx[dx]
        score(n_next, dx_next, to)
        weigh(n, dx, at, before, now)

    def q_wait(dx):
        q_copy(NX - dx).wait_recv()

    score(0, 0, s0)
    q_wait(1)
    step(0, 0, s0, 0, 1, s1)
    stage_own(3)
    stage_own(4)
    q_wait(3)
    step(0, 1, s1, 0, 3, s2)
    stage_opp(1)
    stage_opp(2)
    stage_y(1)
    stage_y(2)
    q_wait(2)
    step(0, 3, s2, 0, 2, s3)
    stage_c(1)
    step(0, 2, s3, 1, 0, s0)
    stage_own(5)
    stage_own(6)
    step(1, 0, s0, 1, 1, s1)
    step(1, 1, s1, 1, 3, s2)
    stage_opp(3)
    stage_opp(4)
    stage_y(3)
    stage_y(4)
    step(1, 3, s2, 1, 2, s3)
    stage_c(2)
    step(1, 2, s3, 2, 2, s0)

    def unit(n, carry):
        step(n, 2, s0, n, 1, s1)

        @pl.when(n == 2)
        def _():
            stage_own(7)

        @pl.when(n == 3)
        def _():
            for m in (5, 6):
                stage_opp(m)
                stage_y(m)

        step(n, 1, s1, n, 3, s2)

        @pl.when(n == 4)
        def _():
            stage_opp(7)
            stage_y(7)

        stage_c(n + 1)
        step(n, 3, s2, n + 1, 2, s0)
        return carry

    lax.fori_loop(2, 6, unit, 0)

    tail = [(n, dx) for dx in WAYS for n in (6, 7)] + [(n, 0) for n in range(2, NZ)]
    at, to = s0, s1
    for i, (n, dx) in enumerate(tail):
        if i == 0:
            stage_c(7)
        if i + 1 < len(tail):
            step(n, dx, at, *tail[i + 1], to)
            at, to = to, at
        else:
            weigh(n, dx, at, mp[dx], mx[dx])
        if n == NZ - 1:
            finish(dx)
            if dx:
                o_copy(dx).start()
    here = dev(x, y, z, 1 - c)
    one = kv.at[z, c, y]

    def sent(send):
        copy(one, one, send, rs.at[z, y], here).wait_send()

    for n in range(1, NZ):
        sent(zs.at[0, n])
    for n in range(NZ):
        both_copy(n).wait_send()

    @pl.when(y >= 2)
    def _():
        for n in range(1, NZ):
            sent(zs.at[1, n])

    @pl.when(y < 2)
    def _():
        sent(yo.at[0])

    @pl.when(y < NY - 1)
    def _():
        for n in range(NZ):
            sent(ys.at[0, n])

    @pl.when(y == 0)
    def _():
        for n in range(NZ):
            sent(ys.at[1, n])

    for dx in WAYS:
        q_copy(dx).wait_send()

    for dx in WAYS:
        o_copy(dx).wait_recv()
    combine()

    for dx in WAYS:
        o_copy(dx).wait_send()


def body(queries, keys, values):
    dma = pltpu.SemaphoreType.DMA
    scratch = [
        pltpu.VMEM(queries.shape, BF16),
        pltpu.VMEM((BLK, HD), BF16),
        pltpu.VMEM((BLK, HD), BF16),
        pltpu.VMEM((NZ, 2, NY, 2 * BLK, HD), BF16),
        pltpu.VMEM((NX, HD, COLS), BF16),
    ]
    scratch += [pltpu.VMEM((2 * BLK * NY, COLS), F32) for _ in range(4)]
    scratch += [pltpu.VMEM((NY, 1, COLS), F32) for _ in range(3)]
    scratch += [
        pltpu.VMEM((NX, HD, COLS), F32),
        pltpu.VMEM((NX, HD + 16, COLS), BF16),
        pltpu.VMEM((NX, HD + 16, COLS), BF16),
        dma((3,)), dma((NZ, NY)), dma((2, NZ)), dma((2, NZ)), dma((1,)), dma((NZ,)), dma((NZ,)),
        dma((NX,)), dma((NX,)), dma((NX,)), dma((NX,)),
    ]
    return pl.pallas_call(
        kernel,
        out_shape=jax.ShapeDtypeStruct(queries.shape, BF16),
        in_specs=[pl.BlockSpec(memory_space=pltpu.HBM)] * 3,
        out_specs=pl.BlockSpec(memory_space=pltpu.VMEM),
        scratch_shapes=scratch,
        compiler_params=pltpu.CompilerParams(
            collective_id=0, has_side_effects=True, vmem_limit_bytes=62 * 1024 * 1024
        ),
    )(queries, keys, values)


def solution(mesh):
    placed = (P("ctx", "head"), P("ctx", None), P("ctx", None))
    return jax.shard_map(
        body, mesh=mesh, in_specs=placed, out_specs=P("ctx", "head"), check_vma=False
    )
```

```python
import math

import jax
import jax.numpy as jnp
from jax import lax
from jax.experimental import pallas as pl
from jax.experimental.pallas import tpu as pltpu
from jax.sharding import PartitionSpec as P

MESH = pl.DeviceIdType.MESH
NX, NY, NZ = 4, 4, 8
BLK = 128
HD = 128
COLS = 512
SCALE = math.log2(math.e) / math.sqrt(HD)
EMPTY = -1e30
HIDDEN = -2e30
WAYS = (2, 1, 3)
RING = {0: (1, 2), 1: (3,), 2: (4,), 3: (5,), 4: (6,)}
OWN_WAY = {**RING, 6: (7,)}
OPP_WAY = {**RING, 5: (7,)}
F32 = jnp.float32
BF16 = jnp.bfloat16


def kernel(
    q_hbm, k_hbm, v_hbm, o_ref,
    q_ref, k_ref, v_ref, kv, qb, s0, s1, s2, s3, mx, mp, ls, acc, osend, orecv,
    ins, rs, zs, ys, yo, ss, sr, qss, qrs, oss, ors,
):
    scores = (s0, s1, s2, s3)
    ctx, x = lax.axis_index("ctx"), lax.axis_index("head")
    c = lax.rem(ctx, 2)
    z = lax.rem(lax.div(ctx, 2), NZ)
    y = lax.div(ctx, 2 * NZ)
    opp = lax.rem(y + 2, NY)
    yup, ydn = lax.rem(y + 1, NY), lax.rem(y + NY - 1, NY)

    def dev(xx, yy, zz, cc):
        return ((yy * NZ + zz) * 2 + cc, xx)

    def copy(src, dst, send, recv, device):
        return pltpu.make_async_remote_copy(
            src_ref=src, dst_ref=dst, send_sem=send, recv_sem=recv, device_id=device, device_id_type=MESH
        )

    rows = pl.ds(pl.multiple_of(x * BLK, BLK), BLK)
    loads = [
        pltpu.make_async_copy(q_hbm, q_ref, ins.at[0]),
        pltpu.make_async_copy(k_hbm.at[rows], k_ref, ins.at[1]),
        pltpu.make_async_copy(v_hbm.at[rows], v_ref, ins.at[2]),
    ]
    for load in loads[::-1]:
        load.start()
    barrier = pltpu.get_barrier_semaphore()
    targets = [dev(lax.rem(x + dx, NX), y, z, c) for dx in WAYS]
    targets += [dev(x, yy, z, c) for yy in (opp, yup, ydn)]
    targets += [dev(x, y, lax.rem(z + d, NZ), c) for d in (1, NZ - 1)] + [dev(x, y, z, 1 - c)]
    for target in targets:
        pl.semaphore_signal(barrier, inc=1, device_id=target, device_id_type=MESH)

    def turn(a):
        return a.astype(F32).T.astype(BF16)

    loads[1].wait()
    kv[z, c, y, :BLK, :] = k_ref[...]
    loads[2].wait()
    kv[z, c, y, BLK:, :] = turn(v_ref[...])

    pl.semaphore_wait(barrier, len(targets))

    def q_copy(dx):
        part = qb.at[x]
        return copy(part, part, qss.at[dx], qrs.at[dx], dev(lax.rem(x + dx, NX), y, z, c))

    def kv_send(zz, yy, send, device):
        part = kv.at[zz, c, yy]
        copy(part, part, send, rs.at[zz, yy], device).start()

    def kv_wait(zz, yy):
        part = kv.at[zz, c, yy]
        copy(part, part, yo.at[0], rs.at[zz, yy], dev(x, y, z, 1 - c)).wait_recv()

    def shift(n):
        d, odd = (n + 1) // 2, n % 2
        return d * (2 * odd - 1)

    def place(n):
        if not isinstance(n, int):
            return lax.rem(z + NZ + lax.div(n + 1, 2) * (2 * lax.rem(n, 2) - 1), NZ)
        return lax.rem(z + NZ + shift(n), NZ)

    def kv_along(item, n):
        zz = place(n)
        for m in (OWN_WAY, OPP_WAY)[item].get(n, ()):
            kv_send(zz, (y, opp)[item], zs.at[item, m], dev(x, y, lax.rem(zz + NZ - shift(m), NZ), c))

    def send_y(n):
        zz = place(n)

        @pl.when(y < NY - 1)
        def _():
            kv_send(zz, y, ys.at[0, n], dev(x, yup, z, c))

        @pl.when(y == 0)
        def _():
            kv_send(zz, y, ys.at[1, n], dev(x, ydn, z, c))

    def stage_own(n):
        zz = place(n)
        kv_wait(zz, y)
        kv_along(0, n)
        send_y(n)

    def stage_opp(n):
        @pl.when(y >= 2)
        def _():
            kv_wait(place(n), opp)
            kv_along(1, n)


    @pl.when(y < 2)
    def _():
        kv_send(z, y, yo.at[0], dev(x, opp, z, c))

    kv_along(0, 0)
    send_y(0)
    loads[0].wait()
    qb[x] = turn(q_ref[...])
    for dx in (1, 3, 2):
        q_copy(dx).start()
    for g in range(NY):
        mx[g] = jnp.full((1, COLS), EMPTY, F32)
        ls[g] = jnp.zeros((1, COLS), F32)
        acc[g] = jnp.zeros((HD, COLS), F32)
    for yy in range(1, NY):

        @pl.when(yy > y)
        def _():
            for zz in range(NZ):
                kv[zz, c, yy] = jnp.zeros((2 * BLK, HD), BF16)


    def both_copy(n):
        zz = place(n)
        part = kv.at[zz, c]
        return copy(part, part, ss.at[n], sr.at[zz], dev(x, y, z, 1 - c))

    def stage_y(n):
        zz = place(n)

        @pl.when(y == NY - 1)
        def _():
            kv_wait(zz, yup)

        @pl.when(y > 0)
        def _():
            kv_wait(zz, ydn)

        both_copy(n).start()

    def stage_c(n):
        zz = place(n)
        part = kv.at[zz, 1 - c]
        copy(part, part, ss.at[0], sr.at[zz], dev(x, y, z, 1 - c)).wait_recv()

    stage_own(1)
    stage_own(2)
    stage_opp(0)
    stage_y(0)
    stage_c(0)

    apart = lax.broadcasted_iota(jnp.int32, (BLK, COLS), 0) - lax.broadcasted_iota(jnp.int32, (BLK, COLS), 1)

    def slab(back):
        return lax.rem(y + NY - back, NY)

    def score(n, dx, to):
        zz, h = place(n), lax.rem(x + dx, NX)
        k = jnp.concatenate([kv[zz, :, slab(back), :BLK, :].reshape(2 * BLK, HD) for back in range(NY)], axis=0)
        s = jnp.dot(k, qb[h], preferred_element_type=F32)
        own = []
        for cc in range(2):
            ahead = (zz - z) * 1024 + (cc - c) * 512 + x * BLK
            own.append(jnp.where(apart <= -ahead, s[cc * BLK:(cc + 1) * BLK], HIDDEN))
        own = jnp.concatenate(own, axis=0)
        to[:2 * BLK] = own
        to[2 * BLK:] = s[2 * BLK:]
        before = mx[dx]
        mp[dx] = before
        top = jnp.maximum(before, jnp.max(own, axis=0, keepdims=True))
        for back in range(1, NY):
            one = jnp.max(s[2 * back * BLK:2 * (back + 1) * BLK], axis=0, keepdims=True)
            top = jnp.maximum(top, jnp.where(back <= y, one, HIDDEN))
        mx[dx] = top

    def weigh(n, dx, at, before, now):
        zz = place(n)
        old = jnp.exp2((before - now) * SCALE)
        now = now * SCALE
        parts = []
        for back in range(NY):
            row = jnp.where(back <= y, now, -HIDDEN) if back else now
            parts.append(jnp.exp2(at[2 * back * BLK:2 * (back + 1) * BLK] * SCALE - row))
        p = jnp.concatenate(parts, axis=0)
        v = jnp.concatenate([kv[zz, cc, slab(back), BLK:, :] for back in range(NY) for cc in range(2)], axis=1)
        ls[dx] = ls[dx] * old + jnp.sum(p, axis=0, keepdims=True)
        acc[dx] = acc[dx] * old + jnp.dot(v, p.astype(BF16), preferred_element_type=F32)

    line = lax.broadcasted_iota(jnp.int32, (16, COLS), 0)

    def thirds(a):
        high = a.astype(BF16).astype(F32)
        mid = (a - high).astype(BF16).astype(F32)
        return high, mid, a - high - mid

    def finish(dx):
        osend[dx, :HD, :] = acc[dx].astype(BF16)
        side = jnp.zeros((16, COLS), F32)
        for i, part in enumerate(thirds(mx[dx]) + thirds(ls[dx])):
            side = jnp.where(line == i, part, side)
        osend[dx, HD:, :] = side.astype(BF16)

    def o_copy(dx):
        h = lax.rem(x + dx, NX)
        return copy(osend.at[dx], orecv.at[dx], oss.at[dx], ors.at[dx], dev(h, y, z, c))

    def combine():
        held = [(osend if dx == 0 else orecv).at[dx] for dx in range(NX)]
        sides = [part[HD:, :].astype(F32) for part in held]
        tops = [side[0:1] + side[1:2] + side[2:3] for side in sides]
        counts = [side[3:4] + side[4:5] + side[5:6] for side in sides]
        top = jnp.maximum(jnp.maximum(tops[0], tops[1]), jnp.maximum(tops[2], tops[3]))
        shares = [jnp.exp2((t - top) * SCALE) for t in tops]
        inverse = 1.0 / sum(share * count for share, count in zip(shares, counts))
        total = sum((share * inverse) * part[:HD, :].astype(F32) for part, share in zip(held, shares))
        o_ref[...] = total.T.astype(BF16)

    def step(n, dx, at, n_next, dx_next, to):
        before, now = mp[dx], mx[dx]
        score(n_next, dx_next, to)
        weigh(n, dx, at, before, now)

    def q_wait(dx):
        q_copy(NX - dx).wait_recv()

    score(0, 0, s0)
    q_wait(1)
    step(0, 0, s0, 0, 1, s1)
    stage_own(3)
    stage_own(4)
    q_wait(3)
    step(0, 1, s1, 0, 3, s2)
    stage_opp(1)
    stage_opp(2)
    stage_y(1)
    stage_y(2)
    q_wait(2)
    step(0, 3, s2, 0, 2, s3)
    stage_c(1)
    step(0, 2, s3, 1, 1, s0)
    stage_own(5)
    stage_own(6)
    step(1, 1, s0, 1, 3, s1)
    stage_opp(3)
    stage_opp(4)
    stage_y(3)
    stage_y(4)
    step(1, 3, s1, 1, 2, s2)
    stage_c(2)
    step(1, 2, s2, 2, 2, s0)

    def unit(n):
        step(n, 2, s0, n, 1, s1)

        @pl.when(n == 2)
        def _():
            stage_own(7)

        @pl.when(n == 3)
        def _():
            for m in (5, 6):
                stage_opp(m)
                stage_y(m)

        step(n, 1, s1, n, 3, s2)

        @pl.when(n == 4)
        def _():
            stage_opp(7)
            stage_y(7)

        stage_c(n + 1)
        step(n, 3, s2, n + 1, 2, s0)

    for n in range(2, 6):
        unit(n)

    tail = [(n, dx) for dx in WAYS for n in (6, 7)] + [(n, 0) for n in range(1, NZ)]
    at, to = s0, s1
    for i, (n, dx) in enumerate(tail):
        if i == 0:
            stage_c(7)
        if i + 1 < len(tail):
            step(n, dx, at, *tail[i + 1], to)
            at, to = to, at
        else:
            weigh(n, dx, at, mp[dx], mx[dx])
        if n == NZ - 1:
            finish(dx)
            if dx:
                o_copy(dx).start()
    here = dev(x, y, z, 1 - c)
    one = kv.at[z, c, y]

    def sent(send):
        copy(one, one, send, rs.at[z, y], here).wait_send()

    for n in range(1, NZ):
        sent(zs.at[0, n])
    for n in range(NZ):
        both_copy(n).wait_send()

    @pl.when(y >= 2)
    def _():
        for n in range(1, NZ):
            sent(zs.at[1, n])

    @pl.when(y < 2)
    def _():
        sent(yo.at[0])

    @pl.when(y < NY - 1)
    def _():
        for n in range(NZ):
            sent(ys.at[0, n])

    @pl.when(y == 0)
    def _():
        for n in range(NZ):
            sent(ys.at[1, n])

    for dx in WAYS:
        q_copy(dx).wait_send()

    for dx in WAYS:
        o_copy(dx).wait_recv()
    combine()

    for dx in WAYS:
        o_copy(dx).wait_send()


def body(queries, keys, values):
    dma = pltpu.SemaphoreType.DMA
    scratch = [
        pltpu.VMEM(queries.shape, BF16),
        pltpu.VMEM((BLK, HD), BF16),
        pltpu.VMEM((BLK, HD), BF16),
        pltpu.VMEM((NZ, 2, NY, 2 * BLK, HD), BF16),
        pltpu.VMEM((NX, HD, COLS), BF16),
    ]
    scratch += [pltpu.VMEM((2 * BLK * NY, COLS), F32) for _ in range(4)]
    scratch += [pltpu.VMEM((NY, 1, COLS), F32) for _ in range(3)]
    scratch += [
        pltpu.VMEM((NX, HD, COLS), F32),
        pltpu.VMEM((NX, HD + 16, COLS), BF16),
        pltpu.VMEM((NX, HD + 16, COLS), BF16),
        dma((3,)), dma((NZ, NY)), dma((2, NZ)), dma((2, NZ)), dma((1,)), dma((NZ,)), dma((NZ,)),
        dma((NX,)), dma((NX,)), dma((NX,)), dma((NX,)),
    ]
    return pl.pallas_call(
        kernel,
        out_shape=jax.ShapeDtypeStruct(queries.shape, BF16),
        in_specs=[pl.BlockSpec(memory_space=pltpu.HBM)] * 3,
        out_specs=pl.BlockSpec(memory_space=pltpu.VMEM),
        scratch_shapes=scratch,
        compiler_params=pltpu.CompilerParams(
            collective_id=0, has_side_effects=True, vmem_limit_bytes=62 * 1024 * 1024
        ),
    )(queries, keys, values)


def solution(mesh):
    placed = (P("ctx", "head"), P("ctx", None), P("ctx", None))
    return jax.shard_map(
        body, mesh=mesh, in_specs=placed, out_specs=P("ctx", "head"), check_vma=False
    )
```

```python
import math

import jax
import jax.numpy as jnp
from jax import lax
from jax.experimental import pallas as pl
from jax.experimental.pallas import tpu as pltpu
from jax.sharding import PartitionSpec as P

MESH = pl.DeviceIdType.MESH
NX, NY, NZ = 4, 4, 8
BLK = 128
HD = 128
COLS = 512
SCALE = math.log2(math.e) / math.sqrt(HD)
EMPTY = -1e30
HIDDEN = -2e30
WAYS = (2, 1, 3)
RING = {0: (1, 2), 1: (3,), 2: (4,), 3: (5,), 4: (6,)}
OWN_WAY = {**RING, 6: (7,)}
OPP_WAY = {**RING, 5: (7,)}
F32 = jnp.float32
BF16 = jnp.bfloat16


def kernel(
    q_hbm, k_hbm, v_hbm, o_ref,
    q_ref, k_ref, v_ref, kv, qb, s0, s1, s2, s3, mx, mp, ls, acc, osend, orecv,
    ins, rs, zs, ys, yo, ss, sr, qss, qrs, oss, ors,
):
    scores = (s0, s1, s2, s3)
    ctx, x = lax.axis_index("ctx"), lax.axis_index("head")
    c = lax.rem(ctx, 2)
    z = lax.rem(lax.div(ctx, 2), NZ)
    y = lax.div(ctx, 2 * NZ)
    opp = lax.rem(y + 2, NY)
    yup, ydn = lax.rem(y + 1, NY), lax.rem(y + NY - 1, NY)

    def dev(xx, yy, zz, cc):
        return ((yy * NZ + zz) * 2 + cc, xx)

    def copy(src, dst, send, recv, device):
        return pltpu.make_async_remote_copy(
            src_ref=src, dst_ref=dst, send_sem=send, recv_sem=recv, device_id=device, device_id_type=MESH
        )

    rows = pl.ds(pl.multiple_of(x * BLK, BLK), BLK)
    loads = [
        pltpu.make_async_copy(q_hbm, q_ref, ins.at[0]),
        pltpu.make_async_copy(k_hbm.at[rows], k_ref, ins.at[1]),
        pltpu.make_async_copy(v_hbm.at[rows], v_ref, ins.at[2]),
    ]
    for load in loads[::-1]:
        load.start()
    barrier = pltpu.get_barrier_semaphore()
    targets = [dev(lax.rem(x + dx, NX), y, z, c) for dx in WAYS]
    targets += [dev(x, yy, z, c) for yy in (opp, yup, ydn)]
    targets += [dev(x, y, lax.rem(z + d, NZ), c) for d in (1, NZ - 1)] + [dev(x, y, z, 1 - c)]
    for target in targets:
        pl.semaphore_signal(barrier, inc=1, device_id=target, device_id_type=MESH)

    def turn(a):
        return a.astype(F32).T.astype(BF16)

    loads[1].wait()
    kv[z, c, y, :BLK, :] = k_ref[...]
    loads[2].wait()
    kv[z, c, y, BLK:, :] = turn(v_ref[...])

    pl.semaphore_wait(barrier, len(targets))

    def q_copy(dx):
        part = qb.at[x]
        return copy(part, part, qss.at[dx], qrs.at[dx], dev(lax.rem(x + dx, NX), y, z, c))

    def kv_send(zz, yy, send, device):
        part = kv.at[zz, c, yy]
        copy(part, part, send, rs.at[zz, yy], device).start()

    def kv_wait(zz, yy):
        part = kv.at[zz, c, yy]
        copy(part, part, yo.at[0], rs.at[zz, yy], dev(x, y, z, 1 - c)).wait_recv()

    def shift(n):
        d, odd = (n + 1) // 2, n % 2
        return d * (2 * odd - 1)

    def place(n):
        if not isinstance(n, int):
            return lax.rem(z + NZ + lax.div(n + 1, 2) * (2 * lax.rem(n, 2) - 1), NZ)
        return lax.rem(z + NZ + shift(n), NZ)

    def kv_along(item, n):
        zz = place(n)
        for m in (OWN_WAY, OPP_WAY)[item].get(n, ()):
            kv_send(zz, (y, opp)[item], zs.at[item, m], dev(x, y, lax.rem(zz + NZ - shift(m), NZ), c))

    def send_y(n):
        zz = place(n)

        @pl.when(y < NY - 1)
        def _():
            kv_send(zz, y, ys.at[0, n], dev(x, yup, z, c))

        @pl.when(y == 0)
        def _():
            kv_send(zz, y, ys.at[1, n], dev(x, ydn, z, c))

    def stage_own(n):
        zz = place(n)
        kv_wait(zz, y)
        kv_along(0, n)
        send_y(n)

    def stage_opp(n):
        @pl.when(y >= 2)
        def _():
            kv_wait(place(n), opp)
            kv_along(1, n)


    @pl.when(y < 2)
    def _():
        kv_send(z, y, yo.at[0], dev(x, opp, z, c))

    kv_along(0, 0)
    send_y(0)
    loads[0].wait()
    qb[x] = turn(q_ref[...])
    for dx in (1, 3, 2):
        q_copy(dx).start()
    for g in range(NY):
        mx[g] = jnp.full((1, COLS), EMPTY, F32)
        ls[g] = jnp.zeros((1, COLS), F32)
        acc[g] = jnp.zeros((HD, COLS), F32)
    for yy in range(1, NY):

        @pl.when(yy > y)
        def _():
            for zz in range(NZ):
                kv[zz, c, yy] = jnp.zeros((2 * BLK, HD), BF16)


    def both_copy(n):
        zz = place(n)
        part = kv.at[zz, c]
        return copy(part, part, ss.at[n], sr.at[zz], dev(x, y, z, 1 - c))

    def stage_y(n):
        zz = place(n)

        @pl.when(y == NY - 1)
        def _():
            kv_wait(zz, yup)

        @pl.when(y > 0)
        def _():
            kv_wait(zz, ydn)

        both_copy(n).start()

    def stage_c(n):
        zz = place(n)
        part = kv.at[zz, 1 - c]
        copy(part, part, ss.at[0], sr.at[zz], dev(x, y, z, 1 - c)).wait_recv()

    stage_own(1)
    stage_own(2)
    stage_opp(0)
    stage_y(0)
    stage_c(0)

    apart = lax.broadcasted_iota(jnp.int32, (BLK, COLS), 0) - lax.broadcasted_iota(jnp.int32, (BLK, COLS), 1)

    def slab(back):
        return lax.rem(y + NY - back, NY)

    def score(n, dx, to):
        zz, h = place(n), lax.rem(x + dx, NX)
        k = jnp.concatenate([kv[zz, :, slab(back), :BLK, :].reshape(2 * BLK, HD) for back in range(NY)], axis=0)
        s = jnp.dot(k, qb[h], preferred_element_type=F32)
        own = s[:2 * BLK]
        if n == 0:
            parts = []
            for cc in range(2):
                ahead = (cc - c) * 512 + x * BLK
                parts.append(jnp.where(apart <= -ahead, s[cc * BLK:(cc + 1) * BLK], HIDDEN))
            own = jnp.concatenate(parts, axis=0)
        to[:2 * BLK] = own
        to[2 * BLK:] = s[2 * BLK:]
        before = mx[dx]
        mp[dx] = before
        one = jnp.max(own, axis=0, keepdims=True)
        top = jnp.maximum(before, jnp.where(zz < z, one, HIDDEN) if n else one)
        for back in range(1, NY):
            one = jnp.max(s[2 * back * BLK:2 * (back + 1) * BLK], axis=0, keepdims=True)
            top = jnp.maximum(top, jnp.where(back <= y, one, HIDDEN))
        mx[dx] = top

    def weigh(n, dx, at, before, now):
        zz = place(n)
        old = jnp.exp2((before - now) * SCALE)
        now = now * SCALE
        parts = []
        for back in range(NY):
            row = now
            if back or n:
                row = jnp.where(back <= y if back else zz < z, now, -HIDDEN)
            parts.append(jnp.exp2(at[2 * back * BLK:2 * (back + 1) * BLK] * SCALE - row))
        p = jnp.concatenate(parts, axis=0)
        v = jnp.concatenate([kv[zz, cc, slab(back), BLK:, :] for back in range(NY) for cc in range(2)], axis=1)
        ls[dx] = ls[dx] * old + jnp.sum(p, axis=0, keepdims=True)
        acc[dx] = acc[dx] * old + jnp.dot(v, p.astype(BF16), preferred_element_type=F32)

    line = lax.broadcasted_iota(jnp.int32, (16, COLS), 0)

    def thirds(a):
        high = a.astype(BF16).astype(F32)
        mid = (a - high).astype(BF16).astype(F32)
        return high, mid, a - high - mid

    def finish(dx):
        osend[dx, :HD, :] = acc[dx].astype(BF16)
        side = jnp.zeros((16, COLS), F32)
        for i, part in enumerate(thirds(mx[dx]) + thirds(ls[dx])):
            side = jnp.where(line == i, part, side)
        osend[dx, HD:, :] = side.astype(BF16)

    def o_copy(dx):
        h = lax.rem(x + dx, NX)
        return copy(osend.at[dx], orecv.at[dx], oss.at[dx], ors.at[dx], dev(h, y, z, c))

    def combine():
        held = [(osend if dx == 0 else orecv).at[dx] for dx in range(NX)]
        sides = [part[HD:, :].astype(F32) for part in held]
        tops = [side[0:1] + side[1:2] + side[2:3] for side in sides]
        counts = [side[3:4] + side[4:5] + side[5:6] for side in sides]
        top = jnp.maximum(jnp.maximum(tops[0], tops[1]), jnp.maximum(tops[2], tops[3]))
        shares = [jnp.exp2((t - top) * SCALE) for t in tops]
        inverse = 1.0 / sum(share * count for share, count in zip(shares, counts))
        total = sum((share * inverse) * part[:HD, :].astype(F32) for part, share in zip(held, shares))
        o_ref[...] = total.T.astype(BF16)

    def step(n, dx, at, n_next, dx_next, to):
        before, now = mp[dx], mx[dx]
        score(n_next, dx_next, to)
        weigh(n, dx, at, before, now)

    def q_wait(dx):
        q_copy(NX - dx).wait_recv()

    score(0, 0, s0)
    q_wait(1)
    step(0, 0, s0, 0, 1, s1)
    stage_own(3)
    stage_own(4)
    q_wait(3)
    step(0, 1, s1, 0, 3, s2)
    stage_opp(1)
    stage_opp(2)
    stage_y(1)
    stage_y(2)
    q_wait(2)
    step(0, 3, s2, 0, 2, s3)
    stage_c(1)
    step(0, 2, s3, 1, 1, s0)
    stage_own(5)
    stage_own(6)
    step(1, 1, s0, 1, 3, s1)
    stage_opp(3)
    stage_opp(4)
    stage_y(3)
    stage_y(4)
    step(1, 3, s1, 1, 2, s2)
    stage_c(2)
    step(1, 2, s2, 2, 2, s0)

    def unit(n):
        step(n, 2, s0, n, 1, s1)

        @pl.when(n == 2)
        def _():
            stage_own(7)

        @pl.when(n == 3)
        def _():
            for m in (5, 6):
                stage_opp(m)
                stage_y(m)

        step(n, 1, s1, n, 3, s2)

        @pl.when(n == 4)
        def _():
            stage_opp(7)
            stage_y(7)

        stage_c(n + 1)
        step(n, 3, s2, n + 1, 2, s0)

    for n in range(2, 6):
        unit(n)

    tail = [(n, dx) for dx in WAYS for n in (6, 7)] + [(n, 0) for n in range(1, NZ)]
    at, to = s0, s1
    for i, (n, dx) in enumerate(tail):
        if i == 0:
            stage_c(7)
        if i + 1 < len(tail):
            step(n, dx, at, *tail[i + 1], to)
            at, to = to, at
        else:
            weigh(n, dx, at, mp[dx], mx[dx])
        if n == NZ - 1:
            finish(dx)
            if dx:
                o_copy(dx).start()
    here = dev(x, y, z, 1 - c)
    one = kv.at[z, c, y]

    def sent(send):
        copy(one, one, send, rs.at[z, y], here).wait_send()

    for n in range(1, NZ):
        sent(zs.at[0, n])
    for n in range(NZ):
        both_copy(n).wait_send()

    @pl.when(y >= 2)
    def _():
        for n in range(1, NZ):
            sent(zs.at[1, n])

    @pl.when(y < 2)
    def _():
        sent(yo.at[0])

    @pl.when(y < NY - 1)
    def _():
        for n in range(NZ):
            sent(ys.at[0, n])

    @pl.when(y == 0)
    def _():
        for n in range(NZ):
            sent(ys.at[1, n])

    for dx in WAYS:
        q_copy(dx).wait_send()

    for dx in WAYS:
        o_copy(dx).wait_recv()
    combine()

    for dx in WAYS:
        o_copy(dx).wait_send()


def body(queries, keys, values):
    dma = pltpu.SemaphoreType.DMA
    scratch = [
        pltpu.VMEM(queries.shape, BF16),
        pltpu.VMEM((BLK, HD), BF16),
        pltpu.VMEM((BLK, HD), BF16),
        pltpu.VMEM((NZ, 2, NY, 2 * BLK, HD), BF16),
        pltpu.VMEM((NX, HD, COLS), BF16),
    ]
    scratch += [pltpu.VMEM((2 * BLK * NY, COLS), F32) for _ in range(4)]
    scratch += [pltpu.VMEM((NY, 1, COLS), F32) for _ in range(3)]
    scratch += [
        pltpu.VMEM((NX, HD, COLS), F32),
        pltpu.VMEM((NX, HD + 16, COLS), BF16),
        pltpu.VMEM((NX, HD + 16, COLS), BF16),
        dma((3,)), dma((NZ, NY)), dma((2, NZ)), dma((2, NZ)), dma((1,)), dma((NZ,)), dma((NZ,)),
        dma((NX,)), dma((NX,)), dma((NX,)), dma((NX,)),
    ]
    return pl.pallas_call(
        kernel,
        out_shape=jax.ShapeDtypeStruct(queries.shape, BF16),
        in_specs=[pl.BlockSpec(memory_space=pltpu.HBM)] * 3,
        out_specs=pl.BlockSpec(memory_space=pltpu.VMEM),
        scratch_shapes=scratch,
        compiler_params=pltpu.CompilerParams(
            collective_id=0, has_side_effects=True, vmem_limit_bytes=62 * 1024 * 1024
        ),
    )(queries, keys, values)


def solution(mesh):
    placed = (P("ctx", "head"), P("ctx", None), P("ctx", None))
    return jax.shard_map(
        body, mesh=mesh, in_specs=placed, out_specs=P("ctx", "head"), check_vma=False
    )
```
